512 devices in a mesh: dp: 16 (over z_lo, x), ctx: 32 (over y, z_hi, core).
Axes of the slice: x: 4, y: 8, z: 8 (z_hi: 2, z_lo: 4; z = z_hi * 4 + z_lo), core: 2. Of those that a mesh axis runs over, the one named last changes fastest.
Arguments:
- queries: bfloat16 [16, 4096, 512], P('dp', 'ctx'), may hold values from -6 to 6
- key_states: bfloat16 [16, 4096, 512], P('dp', 'ctx'), may hold values from -6 to 6
- value_states: bfloat16 [16, 4096, 512], P('dp', 'ctx'), may hold values from -6 to 6
- gate_states: bfloat16 [16, 4096, 512], P('dp', 'ctx'), may hold values from -6 to 6
- out_grad: bfloat16 [16, 4096, 512], P('dp', 'ctx'), may hold values from -6 to 6
- segment_ids: int32 [16, 4096], P('dp'), may hold values from 0 to 3, never falling along the last dimension, each value on 1 to 2048 neighbouring positions
- norm_gain: float32 [512], replicated, may hold values from 0.1 to 1.9
Outputs:
- layer_out: bfloat16 [16, 4096, 512], P('dp', 'ctx')
- query_grad: bfloat16 [16, 4096, 512], P('dp', 'ctx')
- key_grad: bfloat16 [16, 4096, 512], P('dp', 'ctx')
- value_grad: bfloat16 [16, 4096, 512], P('dp', 'ctx')
- gate_grad: bfloat16 [16, 4096, 512], P('dp', 'ctx')
- gain_grad: float32 [512], replicated
The draws below stay inside these ranges and needn't reach their ends.
Inputs may be any that keep to these rules, and one draw needn't show every extreme that they name: `segment_ids`: in each sample the history numbers never fall, each of the 4 histories has 1 to 2048 positions and one has exactly 2048.
All inputs are finite; a program needn't handle non-finite values.
Results may differ from the reference program's by a relative error of at most 0.0058.
Values may be sent and summed in bfloat16 or wider, within the bound.
No kernel may reach another device: no remote copies, remote signals or barrier semaphores. Data moves between devices by JAX's collectives and lax.ppermute only.
A program may use at most 64 MiB of HBM per device.

```python
import math
import jax
import jax.numpy as jnp
import numpy as np
from jax import lax

HEADS = 4
HSIZE = 128
HD = 512
SEQ = 4096
SAMPLES = 16
SEG_COUNT = 4
SEG_MOST = 2048


def level_of(rng, extent, cuts, smallest, high):
    def one(axis_at, blocks):
        steps = jax.random.uniform(jax.random.fold_in(jax.random.fold_in(rng, 6), axis_at), (blocks,), jnp.float32, smallest / len(cuts), high / len(cuts))
        return jnp.repeat(jnp.exp(steps), extent[axis_at] // blocks).reshape((-1,) + (1,) * (len(extent) - axis_at - 1))

    factor_of = one(*cuts[0])
    for cut in cuts[1:]:
        factor_of = factor_of * one(*cut)
    return factor_of


def split_up(count, total, most, slope):
    portions = [(1 << 20) // math.isqrt(standing ** slope) + 1 for standing in range(2, count + 1)]
    rest, counts = total - most - (count - 1), [1] * (count - 1)
    while rest > 0:
        candidates = [i for i in range(count - 1) if counts[i] < most]
        mass, left = sum([portions[i] for i in candidates]), rest
        for i in candidates:
            more = min(most - counts[i], max(1, left * portions[i] // mass), rest)
            counts[i] = counts[i] + more
            rest = rest - more
    return np.array([most] + counts)


def uneven_parts(key, amount, total, limit, skew):
    if amount == 2:
        one = jax.random.randint(key, (), max(1, total - limit), min(limit, total - 1) + 1)
        return jnp.stack([one, total - one])
    tallies = jnp.asarray(split_up(amount, total, limit, skew), jnp.int32)
    twos = (amount - 1) // 2
    giver, receiver = tallies[1:1 + 2 * twos:2], tallies[2:2 + 2 * twos:2]
    slack = jnp.minimum(giver - 1, limit - receiver)
    passed = jax.random.randint(jax.random.fold_in(key, 1), (twos,), 0, 1 << 20) % (slack + 1)
    tallies = tallies.at[1:1 + 2 * twos:2].set(giver - passed).at[2:2 + 2 * twos:2].set(receiver + passed)
    return tallies[jax.random.permutation(jax.random.fold_in(key, 2), amount)]


def normal_values(own_key, extent, spread, reach, split=(), kind=jnp.bfloat16):
    factor_of = level_of(own_key, extent, split, -0.22, 0.18) if split else 1.0
    array = jax.random.normal(own_key, extent, jnp.float32) * spread * factor_of
    return jnp.minimum(jnp.maximum(array, -reach), reach).astype(kind)


def setup_inputs(seed: int = 0) -> dict:
    seeds = jax.random.split(jax.random.key(seed), 8)
    return {
        "queries": normal_values(seeds[0], (SAMPLES, SEQ, HD), 1.0, 6.0, ((0, 16), (1, 32))),
        "key_states": normal_values(seeds[1], (SAMPLES, SEQ, HD), 1.0, 6.0, ((0, 16), (1, 32))),
        "value_states": normal_values(seeds[2], (SAMPLES, SEQ, HD), 1.0, 6.0, ((0, 16), (1, 32))),
        "gate_states": normal_values(seeds[3], (SAMPLES, SEQ, HD), 1.0, 6.0, ((0, 16), (1, 32))),
        "out_grad": normal_values(seeds[4], (SAMPLES, SEQ, HD), 1.0, 6.0, ((0, 16), (1, 32))),
        "segment_ids": jax.vmap(lambda own: jnp.searchsorted(jnp.cumsum(uneven_parts(own, SEG_COUNT, SEQ, SEG_MOST, 0)), jnp.arange(SEQ), side="right"))(jax.random.split(seeds[5], SAMPLES)).reshape((SAMPLES, SEQ)).astype(jnp.int32),
        "norm_gain": jnp.clip(1.0 + 0.18 * jax.random.normal(seeds[6], (HD,), jnp.float32), 0.1, 1.9),
    }


def head_dot(left_rows, right_rows):
    left_heads = left_rows.astype(jnp.float32).reshape(left_rows.shape[0], HEADS, HSIZE)
    right_heads = right_rows.astype(jnp.float32).reshape(right_rows.shape[0], HEADS, HSIZE)
    return jnp.einsum('qhd,khd->hqk', left_heads, right_heads)

def head_product(weights, rows):
    rows_heads = rows.astype(jnp.float32).reshape(rows.shape[0], HEADS, HSIZE)
    result = jnp.einsum('hqk,khd->qhd', weights.astype(jnp.float32), rows_heads)
    return result.reshape(result.shape[0], HEADS * HSIZE)

def head_product_back(weights, rows):
    rows_heads = rows.astype(jnp.float32).reshape(rows.shape[0], HEADS, HSIZE)
    result = jnp.einsum('hqk,qhd->khd', weights.astype(jnp.float32), rows_heads)
    return result.reshape(result.shape[0], HEADS * HSIZE)

def visible_pairs(query_pos, query_seg, key_pos, key_seg):
    return (query_seg[:, None] == key_seg[None, :])[None]

def silu_slope(scores):
    sigmoid = jax.nn.sigmoid(scores)
    return sigmoid * (1.0 + scores * (1.0 - sigmoid))

def reference(queries, key_states, value_states, gate_states, out_grad, segment_ids, norm_gain):
    scale = HSIZE ** (-0.5)
    block = math.gcd(SEQ, 512)
    count = SEQ // block
    block_ids = jnp.arange(count, dtype=jnp.int32)
    positions = jnp.arange(SEQ, dtype=jnp.int32)

    def one_sample(items):
        query_all, key_all, value_all, gate_all, grad_all, segs = items

        def forward_block(block_id):
            first = block_id * block
            query_block = lax.dynamic_slice_in_dim(query_all, first, block, 0)
            query_pos = lax.dynamic_slice_in_dim(positions, first, block, 0)
            query_seg = lax.dynamic_slice_in_dim(segs, first, block, 0)
            scores = scale * head_dot(query_block, key_all)
            visible = visible_pairs(query_pos, query_seg, positions, segs)
            weights = jnp.where(visible, jax.nn.silu(scores), 0.0).astype(jnp.bfloat16)
            return head_product(weights, value_all)
        attended = lax.map(forward_block, block_ids).reshape(SEQ, HD)
        inv_rms = lax.rsqrt(lax.optimization_barrier(jnp.mean(attended * attended, axis=1, keepdims=True)) + 1e-06)
        normed = attended * inv_rms
        gain_row = norm_gain[None, :]
        gate_f = gate_all.astype(jnp.float32)
        grad_f = grad_all.astype(jnp.float32)
        layer_out = (normed * gain_row * gate_f).astype(jnp.bfloat16)
        gate_grad = (grad_f * normed * gain_row).astype(jnp.bfloat16)
        gain_part = lax.optimization_barrier(jnp.sum(grad_f * normed * gate_f, axis=0))
        normed_grad = grad_f * gain_row * gate_f
        attn_grad = (inv_rms * (normed_grad - normed * lax.optimization_barrier(jnp.mean(normed * normed_grad, axis=1, keepdims=True)))).astype(jnp.bfloat16)

        def query_block_grad(block_id):
            first = block_id * block
            query_block = lax.dynamic_slice_in_dim(query_all, first, block, 0)
            grad_block = lax.dynamic_slice_in_dim(attn_grad, first, block, 0)
            query_pos = lax.dynamic_slice_in_dim(positions, first, block, 0)
            query_seg = lax.dynamic_slice_in_dim(segs, first, block, 0)
            scores = scale * head_dot(query_block, key_all)
            visible = visible_pairs(query_pos, query_seg, positions, segs)
            value_dot = head_dot(grad_block, value_all)
            slopes = jnp.where(visible, scale * value_dot * silu_slope(scores), 0.0).astype(jnp.bfloat16)
            return head_product(slopes, key_all)
        query_grad = lax.map(query_block_grad, block_ids).reshape(SEQ, HD)

        def key_block_grad(block_id):
            first = block_id * block
            key_block = lax.dynamic_slice_in_dim(key_all, first, block, 0)
            value_block = lax.dynamic_slice_in_dim(value_all, first, block, 0)
            key_pos = lax.dynamic_slice_in_dim(positions, first, block, 0)
            key_seg = lax.dynamic_slice_in_dim(segs, first, block, 0)
            scores = scale * head_dot(query_all, key_block)
            visible = visible_pairs(positions, segs, key_pos, key_seg)
            weights = jnp.where(visible, jax.nn.silu(scores), 0.0).astype(jnp.bfloat16)
            value_dot = head_dot(attn_grad, value_block)
            slopes = jnp.where(visible, scale * value_dot * silu_slope(scores), 0.0).astype(jnp.bfloat16)
            return (head_product_back(slopes, query_all), head_product_back(weights, attn_grad))
        key_parts, value_parts = lax.map(key_block_grad, block_ids)
        key_grad = key_parts.reshape(SEQ, HD)
        value_grad = value_parts.reshape(SEQ, HD)
        return (layer_out, query_grad.astype(jnp.bfloat16), key_grad.astype(jnp.bfloat16), value_grad.astype(jnp.bfloat16), gate_grad, gain_part)
    results = lax.map(one_sample, (queries, key_states, value_states, gate_states, out_grad, segment_ids))
    gain_grad = lax.optimization_barrier(jnp.sum(results[5], axis=0)) / math.sqrt(SAMPLES * SEQ)
    return (results[0], results[1], results[2], results[3], results[4], gain_grad)
```

```python
import functools
import math

import jax
import jax.numpy as jnp
from jax import lax
from jax.experimental import pallas as pl
from jax.experimental.pallas import tpu as pltpu
from jax.sharding import PartitionSpec as P

HEADS = 4
HSIZE = 128
HD = 512
ROWS = 128
QUAD = 4
RING = 8
TILE = QUAD * ROWS
HALF = TILE // 2
SCALE = HSIZE ** (-0.5)
CHUNK = 256
NT = (((1,), (1,)), ((), ()))
NN = (((1,), (0,)), ((), ()))
TN = (((0,), (0,)), ((), ()))
VMEM_LIMIT = 48 * 1024 * 1024
OFFSETS = (0, -1, 1, -2, 2, -3, 3, 4)


def dot(left, right, dims):
    return lax.dot_general(left, right, dims, preferred_element_type=jnp.float32)


def along_y(value, step):
    return lax.ppermute(
        value,
        "ctx",
        [
            (y * QUAD + c, ((y + step) % RING) * QUAD + c)
            for y in range(RING)
            for c in range(QUAD)
        ],
    )


def in_quad(value, flip):
    return lax.ppermute(
        value,
        "ctx",
        [(y * QUAD + c, y * QUAD + (c ^ flip)) for y in range(RING) for c in range(QUAD)],
    )


def block_of(refs, offset, which):
    if offset < 7:
        return refs[offset][which]
    return jnp.concatenate([refs[7][which], refs[8][which]], axis=0)


def head(h):
    return slice(h * HSIZE, (h + 1) * HSIZE)


def forward_kernel(info, qseg, kseg, q, *rest):
    kv, (keep, send, acc) = rest[:9], rest[9:]
    y = info[0]
    acc[...] = jnp.zeros_like(acc)
    for r, off in enumerate(OFFSETS):
        yy = lax.rem(y + (off + RING), RING)

        @pl.when(info[1 + r] > 0)
        def _(r=r, yy=yy):
            krow = kseg[pl.ds(yy, 1), :]
            for h in range(HEADS):
                kb = block_of(kv, r, 0)[:, head(h)]
                vb = block_of(kv, r, 1)[:, head(h)]
                for c in range(TILE // CHUNK):
                    rows = slice(c * CHUNK, (c + 1) * CHUNK)
                    half = dot(q[rows, head(h)], kb, NT) * (0.5 * SCALE)
                    silu = half + half * jnp.tanh(half)
                    w = jnp.where(qseg[rows, :] == krow, silu, 0.0).astype(jnp.bfloat16)
                    acc[rows, head(h)] += dot(w, vb, NN)

    keep[...] = acc[:HALF, :]
    send[...] = acc[HALF:, :].astype(jnp.bfloat16)


def norm_kernel(mine, other, gate, grad, gain, out, gate_grad, attn_grad, part):
    att = mine[...] + other[...].astype(jnp.float32)
    inv = lax.rsqrt(jnp.mean(att * att, axis=1, keepdims=True) + 1e-06)
    normed = att * inv
    g = gain[...]
    gate_f = gate[0].astype(jnp.float32)
    grad_f = grad[0].astype(jnp.float32)
    out[0] = (normed * g * gate_f).astype(jnp.bfloat16)
    gate_grad[0] = (grad_f * normed * g).astype(jnp.bfloat16)
    both = grad_f * gate_f
    part[...] = jnp.broadcast_to(jnp.sum(both * normed, axis=0, keepdims=True), part.shape)
    ng = both * g
    mean = jnp.mean(normed * ng, axis=1, keepdims=True)
    attn_grad[...] = (inv * (ng - normed * mean)).astype(jnp.bfloat16)


def backward_kernel(info, qseg, kseg, q, da, *rest):
    kv, (keep, send, dkv, acc, dk, dv) = rest[:9], rest[9:]
    y = info[0]
    acc[...] = jnp.zeros_like(acc)
    for r, off in enumerate(OFFSETS):
        yy = lax.rem(y + (off + RING), RING)

        @pl.when(info[1 + r] > 0)
        def _(r=r, yy=yy):
            krow = kseg[pl.ds(yy, 1), :]
            for h in range(HEADS):
                kb = block_of(kv, r, 0)[:, head(h)]
                vb = block_of(kv, r, 1)[:, head(h)]
                for c in range(TILE // CHUNK):
                    rows = slice(c * CHUNK, (c + 1) * CHUNK)
                    qb = q[rows, head(h)]
                    db = da[rows, head(h)]
                    half = dot(qb, kb, NT) * (0.5 * SCALE)
                    vd = dot(db, vb, NT)
                    t = jnp.tanh(half)
                    seen = qseg[rows, :] == krow
                    w = jnp.where(seen, half + half * t, 0.0).astype(jnp.bfloat16)
                    bend = 1.0 + half * (1.0 - t)
                    slope = (0.5 * SCALE) * vd * (1.0 + t) * bend
                    slope = jnp.where(seen, slope, 0.0).astype(jnp.bfloat16)
                    acc[rows, head(h)] += dot(slope, kb, NN)
                    dk_part = dot(slope, qb, TN)
                    dv_part = dot(w, db, TN)
                    if c == 0:
                        dk[:, head(h)] = dk_part
                        dv[:, head(h)] = dv_part
                    else:
                        dk[:, head(h)] += dk_part
                        dv[:, head(h)] += dv_part
            dkv[yy, 0] = dk[...].astype(jnp.bfloat16)
            dkv[yy, 1] = dv[...].astype(jnp.bfloat16)

        @pl.when(info[1 + r] == 0)
        def _(yy=yy):
            dkv[yy] = jnp.zeros((2, ROWS, HD), jnp.bfloat16)

    keep[...] = acc[:HALF, :]
    send[...] = acc[HALF:, :].astype(jnp.bfloat16)


def vmem(count):
    return [pl.BlockSpec(memory_space=pltpu.VMEM)] * count


def smem():
    return [pl.BlockSpec(memory_space=pltpu.SMEM)]


def params():
    return pltpu.CompilerParams(vmem_limit_bytes=VMEM_LIMIT)


def per_device(queries, key_states, value_states, gate_states, out_grad, segment_ids, norm_gain):
    place = lax.axis_index("ctx")
    y, quad = place // QUAD, lax.rem(place, QUAD)
    kv = jnp.concatenate([key_states, value_states], axis=0)

    q_pair = jnp.concatenate([queries[0], in_quad(queries[0], 2)], axis=0)
    q_tile = jnp.concatenate([q_pair, in_quad(q_pair, 1)], axis=0)

    up = down = kv
    blocks = [kv]
    for _ in range(3):
        up, down = along_y(up, 1), along_y(down, -1)
        blocks += [up, down]
    blocks += [along_y(up[:, : ROWS // 2], 1), along_y(down[:, ROWS // 2 :], -1)]

    segs = segment_ids.reshape(RING, QUAD, ROWS)
    kseg = lax.dynamic_index_in_dim(segs, quad, 1, keepdims=False)
    own = lax.dynamic_index_in_dim(segs, y, 0, keepdims=False)
    qseg = jnp.concatenate(
        [lax.dynamic_index_in_dim(own, quad ^ flip, 0, keepdims=False) for flip in (0, 2, 1, 3)]
    )
    low, high = own[0, 0], own[QUAD - 1, ROWS - 1]
    qseg = jnp.broadcast_to(qseg[:, None], (TILE, HSIZE))
    seen = ((kseg[:, 0] <= high) & (kseg[:, ROWS - 1] >= low)).astype(jnp.int32)
    seen = jnp.stack(
        [lax.dynamic_index_in_dim(seen, lax.rem(y + (off + RING), RING), 0, False) for off in OFFSETS]
    )
    info = jnp.concatenate([y.astype(jnp.int32)[None], seen])

    keep, send = pl.pallas_call(
        forward_kernel,
        out_shape=(
            jax.ShapeDtypeStruct((HALF, HD), jnp.float32),
            jax.ShapeDtypeStruct((HALF, HD), jnp.bfloat16),
        ),
        in_specs=smem() + vmem(12),
        out_specs=tuple(vmem(2)),
        scratch_shapes=[pltpu.VMEM((TILE, HD), jnp.float32)],
        compiler_params=params(),
        name="forward_tile",
    )(info, qseg, kseg, q_tile, *blocks)
    keep = keep + in_quad(send, 1).astype(jnp.float32)
    mine, send = keep[:ROWS], keep[ROWS:].astype(jnp.bfloat16)
    other = in_quad(send, 2)

    row = jax.ShapeDtypeStruct((1, ROWS, HD), jnp.bfloat16)
    layer_out, gate_grad, attn_grad, part = pl.pallas_call(
        norm_kernel,
        out_shape=(
            row,
            row,
            jax.ShapeDtypeStruct((ROWS, HD), jnp.bfloat16),
            jax.ShapeDtypeStruct((8, HD), jnp.float32),
        ),
        in_specs=vmem(5),
        out_specs=tuple(vmem(4)),
        compiler_params=params(),
        name="norm_rows",
    )(mine, other, gate_states, out_grad, norm_gain[None, :])

    grad_pair = jnp.concatenate([attn_grad, in_quad(attn_grad, 2)], axis=0)
    grad_tile = jnp.concatenate([grad_pair, in_quad(grad_pair, 1)], axis=0)

    keep, send, dkv = pl.pallas_call(
        backward_kernel,
        out_shape=(
            jax.ShapeDtypeStruct((HALF, HD), jnp.float32),
            jax.ShapeDtypeStruct((HALF, HD), jnp.bfloat16),
            jax.ShapeDtypeStruct((RING, 2, ROWS, HD), jnp.bfloat16),
        ),
        in_specs=smem() + vmem(13),
        out_specs=tuple(vmem(3)),
        scratch_shapes=[
            pltpu.VMEM((TILE, HD), jnp.float32),
            pltpu.VMEM((ROWS, HD), jnp.float32),
            pltpu.VMEM((ROWS, HD), jnp.float32),
        ],
        compiler_params=params(),
        name="backward_tile",
    )(info, qseg, kseg, q_tile, grad_tile, *blocks)

    parts = lax.all_to_all(
        dkv,
        "ctx",
        split_axis=0,
        concat_axis=0,
        tiled=True,
        axis_index_groups=[[y * QUAD + c for y in range(RING)] for c in range(QUAD)],
    )
    keep = keep + in_quad(send, 1).astype(jnp.float32)
    mine, send = keep[:ROWS], keep[ROWS:].astype(jnp.bfloat16)
    query_grad = (mine + in_quad(send, 2).astype(jnp.float32)).astype(jnp.bfloat16)
    total = jnp.sum(parts.astype(jnp.float32), axis=0).astype(jnp.bfloat16)

    gain_sum = part[:1]
    for flip in (1, 2):
        gain_sum = gain_sum + in_quad(gain_sum, flip)
    for flip in (1, 2, 4):
        gain_sum = gain_sum + lax.ppermute(
            gain_sum,
            "ctx",
            [(i, i ^ (flip * QUAD)) for i in range(RING * QUAD)],
        )
    dp = lax.axis_size("dp")
    flip = 1
    while flip < dp:
        gain_sum = gain_sum + lax.ppermute(gain_sum, "dp", [(i, i ^ flip) for i in range(dp)])
        flip *= 2
    gain_grad = gain_sum[0] / math.sqrt(dp * RING * QUAD * ROWS)

    return (
        layer_out,
        query_grad[None],
        total[:1],
        total[1:],
        gate_grad,
        gain_grad,
    )


def solution(mesh):
    rows = P("dp", "ctx", None)
    return jax.shard_map(
        per_device,
        mesh=mesh,
        in_specs=(rows, rows, rows, rows, rows, P("dp", None), P()),
        out_specs=(rows, rows, rows, rows, rows, P()),
        check_vma=False,
    )
```

```python
import math

import jax
import jax.numpy as jnp
from jax import lax
from jax.experimental import pallas as pl
from jax.experimental.pallas import tpu as pltpu
from jax.sharding import PartitionSpec as P

HEADS = 4
HSIZE = 128
HD = 512
ROWS = 128
QUAD = 4
RING = 8
CTX = QUAD * RING
TILE = QUAD * ROWS
HALF = TILE // 2
CUT = ROWS // 2
SCALE = HSIZE ** (-0.5)
CHUNK = 256
CORE, ZHI = 1, 2
NT = (((1,), (1,)), ((), ()))
NN = (((1,), (0,)), ((), ()))
TN = (((0,), (0,)), ((), ()))
VMEM_LIMIT = 16 * 1024 * 1024
BF16, F32 = jnp.bfloat16, jnp.float32
OFFSETS = (0, -1, 1, -2, 2, -3, 3, 4)
QUADS = [[y * QUAD + c for c in range(QUAD)] for y in range(RING)]
RINGS = [[y * QUAD + c for y in range(RING)] for c in range(QUAD)]


def dot(left, right, dims):
    return lax.dot_general(left, right, dims, preferred_element_type=F32)


def along(value, step):
    return lax.ppermute(value, "ctx", [(i, (i + step * QUAD) % CTX) for i in range(CTX)])


def swap(value, flip):
    return lax.ppermute(value, "ctx", [(i, i ^ flip) for i in range(CTX)])


def everywhere(value, axis, groups, size):
    value = jnp.broadcast_to(value, (size,) + value.shape[1:])
    return lax.all_to_all(value, axis, 0, 0, tiled=True, axis_index_groups=groups)


def head(h):
    return slice(h * HSIZE, (h + 1) * HSIZE)


def block_of(kv, r, which):
    if r < RING - 1:
        return kv[r][which]
    return jnp.concatenate([kv[RING - 1][which], kv[RING][which]], axis=0)


def meets(ends, place, block):
    first = (place // QUAD) * QUAD
    return (ends[block, 0] <= ends[first + QUAD - 1, 1]) & (ends[block, 1] >= ends[first, 0])


def key_block(place, offset):
    return lax.rem(place + (offset + RING) * QUAD, CTX)


def pack_kernel(queries, keys, values, kv, twice, sems):
    copies = [
        pltpu.make_async_copy(source.at[0], target, sems.at[i])
        for i, (source, target) in enumerate(
            ((keys, kv.at[0]), (values, kv.at[1]), (queries, twice.at[0]), (queries, twice.at[1]))
        )
    ]
    for copy in copies:
        copy.start()
    for copy in copies:
        copy.wait()


def order_kernel(place, segs, queries, qseg, q):
    for i, flip in enumerate((0, ZHI, CORE, CORE + ZHI)):
        rows = slice(i * ROWS, (i + 1) * ROWS)
        row = segs[pl.ds(place[0] ^ flip, 1), :]
        qseg[rows, :] = jnp.broadcast_to(row, (ROWS, ROWS)).T
        q[rows, :] = queries[lax.rem(place[0], QUAD) ^ flip, 0]


def forward_kernel(place, ends, qseg, segs, q, *rest):
    kv, (keep, send, acc) = rest[: RING + 1], rest[RING + 1 :]
    acc[...] = jnp.zeros_like(acc)
    for r, offset in enumerate(OFFSETS):
        block = key_block(place[0], offset)

        @pl.when(meets(ends, place[0], block))
        def _(r=r, block=block):
            krow = segs[pl.ds(block, 1), :]
            for h in range(HEADS):
                kb = block_of(kv, r, 0)[:, head(h)]
                vb = block_of(kv, r, 1)[:, head(h)]
                for c in range(TILE // CHUNK):
                    rows = slice(c * CHUNK, (c + 1) * CHUNK)
                    half = dot(q[rows, head(h)], kb, NT) * (0.5 * SCALE)
                    silu = half + half * jnp.tanh(half)
                    w = jnp.where(qseg[rows, :] == krow, silu, 0.0).astype(BF16)
                    acc[rows, head(h)] += dot(w, vb, NN)

    keep[...] = acc[:HALF, :]
    send[...] = acc[HALF:, :].astype(BF16)


def norm_kernel(kept, came, gate, grad, gain, out, gate_grad, attn_grad, part):
    g = gain[...]
    att = kept[...] + came[...].astype(F32)
    inv = lax.rsqrt(jnp.mean(att * att, axis=1, keepdims=True) + 1e-06)
    normed = att * inv
    gate_f = gate[0].astype(F32)
    grad_f = grad[0].astype(F32)
    both = grad_f * gate_f
    out[0] = (normed * g * gate_f).astype(BF16)
    gate_grad[0] = (grad_f * normed * g).astype(BF16)
    part[...] = jnp.sum(both * normed, axis=0, keepdims=True)
    ng = both * g
    mean = jnp.mean(normed * ng, axis=1, keepdims=True)
    attn_grad[...] = (inv * (ng - normed * mean)).astype(BF16)


def backward_kernel(place, ends, qseg, segs, q, da, *rest):
    kv, (keep, send, dkv, acc, dk, dv) = rest[: RING + 1], rest[RING + 1 :]
    acc[...] = jnp.zeros_like(acc)
    for r, offset in enumerate(OFFSETS):
        block = key_block(place[0], offset)
        row = pl.multiple_of((block // QUAD) * (2 * ROWS), 2 * ROWS)
        seen = meets(ends, place[0], block)

        @pl.when(seen)
        def _(r=r, block=block, row=row):
            krow = segs[pl.ds(block, 1), :]
            for h in range(HEADS):
                kb = block_of(kv, r, 0)[:, head(h)]
                vb = block_of(kv, r, 1)[:, head(h)]
                for c in range(TILE // CHUNK):
                    rows = slice(c * CHUNK, (c + 1) * CHUNK)
                    qb, db = q[rows, head(h)], da[rows, head(h)]
                    half = dot(qb, kb, NT) * (0.5 * SCALE)
                    vd = dot(db, vb, NT)
                    t = jnp.tanh(half)
                    same = qseg[rows, :] == krow
                    w = jnp.where(same, half + half * t, 0.0).astype(BF16)
                    slope = (0.5 * SCALE) * vd * (1.0 + t) * (1.0 + half * (1.0 - t))
                    slope = jnp.where(same, slope, 0.0).astype(BF16)
                    acc[rows, head(h)] += dot(slope, kb, NN)
                    dk_part = dot(slope, qb, TN)
                    dv_part = dot(w, db, TN)
                    if c == 0:
                        dk[:, head(h)] = dk_part
                        dv[:, head(h)] = dv_part
                    else:
                        dk[:, head(h)] += dk_part
                        dv[:, head(h)] += dv_part
            dkv[pl.ds(row, ROWS), :] = dk[...].astype(BF16)
            dkv[pl.ds(row + ROWS, ROWS), :] = dv[...].astype(BF16)

        @pl.when(jnp.logical_not(seen))
        def _(row=row):
            dkv[pl.ds(row, 2 * ROWS), :] = jnp.zeros((2 * ROWS, HD), BF16)

    keep[...] = acc[:HALF, :]
    send[...] = acc[HALF:, :].astype(BF16)


def call(kernel, name, outs, operands, scalars=0, scratch=(), us=1):
    return pl.pallas_call(
        kernel,
        out_shape=tuple(jax.ShapeDtypeStruct(shape, dtype) for shape, dtype in outs),
        in_specs=[pl.BlockSpec(memory_space=pltpu.SMEM)] * scalars
        + [pl.BlockSpec(memory_space=pltpu.VMEM)] * (len(operands) - scalars),
        out_specs=(pl.BlockSpec(memory_space=pltpu.VMEM),) * len(outs),
        scratch_shapes=[pltpu.VMEM(shape, F32) for shape in scratch],
        compiler_params=pltpu.CompilerParams(vmem_limit_bytes=VMEM_LIMIT),
        cost_estimate=pl.CostEstimate(
            flops=us * 500_000_000, bytes_accessed=us * 1_000_000, transcendentals=0
        ),
        name=name,
    )(*operands)


def after(value, *others):
    return lax.optimization_barrier((value, *others))[0]


def sum_quad(keep, send):
    keep = keep + swap(send, CORE).astype(F32)
    return keep[:ROWS], swap(keep[ROWS:].astype(BF16), ZHI)


def per_device(queries, key_states, value_states, gate_states, out_grad, segment_ids, norm_gain):
    place = lax.axis_index("ctx").astype(jnp.int32)
    rows, tile, half = (1, ROWS, HD), (TILE, HD), (HALF, HD)
    pair = jax.ShapeDtypeStruct((2, ROWS, HD), BF16)
    kv, twice = pl.pallas_call(
        pack_kernel,
        out_shape=(pair, pair),
        in_specs=[pl.BlockSpec(memory_space=pl.ANY)] * 3,
        out_specs=(pl.BlockSpec(memory_space=pltpu.VMEM),) * 2,
        scratch_shapes=[pltpu.SemaphoreType.DMA((4,))],
        compiler_params=pltpu.CompilerParams(vmem_limit_bytes=VMEM_LIMIT),
        name="pack_rows",
    )(queries, key_states, value_states)
    gathered = lax.all_gather(twice, "ctx", axis_index_groups=QUADS)

    up = down = kv
    blocks = [kv]
    for _ in range(2):
        up, down = along(up, 1), along(down, -1)
        blocks += [up, down]
    blocks += [along(up, 1), along(down, -1), along(up[:, :CUT], 2), along(down[:, CUT:], -2)]

    segs = segment_ids.reshape(CTX, ROWS)
    ends = segs[:, :: ROWS - 1]
    qseg, q_tile = call(
        order_kernel,
        "order_rows",
        [((TILE, ROWS), jnp.int32), (tile, BF16)],
        (place[None], segs, gathered),
        1,
    )
    shared = (place[None], ends, qseg, segs, q_tile)

    keep, send = call(
        forward_kernel,
        "forward_tile",
        [(half, F32), (half, BF16)],
        (*shared, *blocks),
        2,
        [tile],
        us=3,
    )
    mine, came = sum_quad(keep, send)
    layer_out, gate_grad, attn_grad, part = call(
        norm_kernel,
        "norm_rows",
        [(rows, BF16), (rows, BF16), ((ROWS, HD), BF16), ((1, HD), F32)],
        (mine, came, gate_states, out_grad, norm_gain[None, :]),
    )
    part = jnp.sum(everywhere(part, "ctx", RINGS, RING), axis=0, keepdims=True)
    grad_tile = jnp.concatenate([attn_grad, swap(attn_grad, ZHI)], axis=0)
    grad_tile = after(grad_tile, part)
    grad_tile = jnp.concatenate([grad_tile, swap(grad_tile, CORE)], axis=0)

    keep, send, dkv = call(
        backward_kernel,
        "backward_tile",
        [(half, F32), (half, BF16), ((RING * 2 * ROWS, HD), BF16)],
        (*shared, grad_tile, *blocks),
        2,
        [tile, (ROWS, HD), (ROWS, HD)],
        us=9,
    )
    dkv_sum = lax.psum_scatter(dkv, "ctx", tiled=True, axis_index_groups=RINGS)
    mine, came = sum_quad(keep, send)
    query_grad = (mine + came.astype(F32)).astype(BF16)

    dp = lax.axis_size("dp")
    part = after(part, query_grad)
    part = jnp.sum(everywhere(part, "ctx", QUADS, QUAD), axis=0, keepdims=True)
    part = jnp.sum(everywhere(part, "dp", None, dp), axis=0)
    gain_grad = part / math.sqrt(dp * CTX * ROWS)

    return (
        layer_out,
        query_grad[None],
        dkv_sum[None, :ROWS],
        dkv_sum[None, ROWS:],
        gate_grad,
        gain_grad,
    )


def solution(mesh):
    rows = P("dp", "ctx", None)
    return jax.shard_map(
        per_device,
        mesh=mesh,
        in_specs=(rows, rows, rows, rows, rows, P("dp", None), P()),
        out_specs=(rows, rows, rows, rows, rows, P()),
        check_vma=False,
    )
```

```python
import math

import jax
import jax.numpy as jnp
from jax import lax
from jax.experimental import pallas as pl
from jax.experimental.pallas import tpu as pltpu
from jax.sharding import PartitionSpec as P

HEADS = 4
HSIZE = 128
HD = 512
ROWS = 128
QUAD = 4
RING = 8
CTX = QUAD * RING
TILE = QUAD * ROWS
HALF = TILE // 2
CUT = ROWS // 2
SCALE = HSIZE ** (-0.5)
CHUNK = 256
CORE, ZHI = 1, 2
NT = (((1,), (1,)), ((), ()))
NN = (((1,), (0,)), ((), ()))
TN = (((0,), (0,)), ((), ()))
VMEM_LIMIT = 16 * 1024 * 1024
BF16, F32 = jnp.bfloat16, jnp.float32
EXTRA = 16
PAIRS = (((0, 0), (-1, 1)), ((1, 2), (2, 4)), ((-2, 3), (-3, 5)), ((3, 6), (4, 7)))
QUADS = [[y * QUAD + c for c in range(QUAD)] for y in range(RING)]
ZPAIRS = [[y * QUAD + z * ZHI + c for z in range(2)] for y in range(RING) for c in range(2)]
RINGS = [[y * QUAD + c for y in range(RING)] for c in range(QUAD)]


def dot(left, right, dims):
    return lax.dot_general(left, right, dims, preferred_element_type=F32)


def along(value, step):
    return lax.ppermute(value, "ctx", [(i, (i + step * QUAD) % CTX) for i in range(CTX)])


def swap(value, flip):
    return lax.ppermute(value, "ctx", [(i, i ^ flip) for i in range(CTX)])


def everywhere(value, axis, groups, size):
    value = jnp.broadcast_to(value, (size,) + value.shape[1:])
    return lax.all_to_all(value, axis, 0, 0, tiled=True, axis_index_groups=groups)


def head(h):
    return slice(h * HSIZE, (h + 1) * HSIZE)


def pair_of(kv, pair, which, h):
    parts = []
    for _, at in PAIRS[pair]:
        for ref in kv[at:] if at == RING - 1 else kv[at : at + 1]:
            parts.append(ref[which, :, head(h)])
    return jnp.concatenate(parts, axis=0)


def key_blocks(place, pair):
    return [lax.rem(place + (offset + RING) * QUAD, CTX) for offset, _ in PAIRS[pair]]


def meets(ends, place, c, blocks):
    first = (place // QUAD) * QUAD + c * (CHUNK // ROWS)
    low, high = ends[first, 0], ends[first + CHUNK // ROWS - 1, 1]
    hits = [(ends[block, 0] <= high) & (ends[block, 1] >= low) for block in blocks]
    return hits[0] | hits[1]


def same_history(qseg, segs, rows, blocks):
    krow = jnp.concatenate([segs[pl.ds(block, 1), :] for block in blocks], axis=1)
    return jnp.concatenate([qseg[rows, :]] * 2, axis=1) == krow


def rows_of(place, flip):
    quad = lax.rem(place, QUAD) ^ flip
    return pl.ds(pl.multiple_of(quad * ROWS, ROWS), ROWS)


def share_out(place, acc, keep, send):
    for i, flip in enumerate((0, ZHI)):
        rows = slice(i * ROWS, (i + 1) * ROWS)
        keep[rows, :] = acc[rows_of(place, flip), :]
        send[rows, :] = acc[rows_of(place, flip ^ CORE), :].astype(BF16)


def segment_kernel(place, segs, qseg):
    first = (place[0] // QUAD) * QUAD
    for i in range(QUAD):
        row = segs[pl.ds(first + i, 1), :]
        qseg[i * ROWS : (i + 1) * ROWS, :] = jnp.broadcast_to(row, (ROWS, ROWS)).T


def queries_of(q, c, h):
    return q[2 * c : 2 * c + 2, 0, :, head(h)].reshape(CHUNK, HSIZE)


def forward_kernel(place, ends, qseg, segs, q, *rest):
    kv, (keep, send, acc) = rest[: RING + 1], rest[RING + 1 :]
    acc[...] = jnp.zeros_like(acc)
    for pair in range(len(PAIRS)):
        blocks = key_blocks(place[0], pair)
        for c in range(TILE // CHUNK):

            @pl.when(meets(ends, place[0], c, blocks))
            def _(pair=pair, blocks=blocks, c=c):
                rows = slice(c * CHUNK, (c + 1) * CHUNK)
                same = same_history(qseg, segs, rows, blocks)
                for h in range(HEADS):
                    keys, values = pair_of(kv, pair, 0, h), pair_of(kv, pair, 1, h)
                    half = dot(queries_of(q, c, h), keys, NT) * (0.5 * SCALE)
                    silu = half + half * jnp.tanh(half)
                    w = jnp.where(same, silu, 0.0).astype(BF16)
                    acc[rows, head(h)] += dot(w, values, NN)

    share_out(place[0], acc, keep, send)


def norm_kernel(place, kept, came, gate, grad, gain, out, gate_grad, attn_grad):
    g = gain[...]
    att = kept[...] + came[1 - lax.rem(place[0], QUAD) // ZHI].astype(F32)
    inv = lax.rsqrt(jnp.mean(att * att, axis=1, keepdims=True) + 1e-06)
    normed = att * inv
    gate_f = gate[0].astype(F32)
    grad_f = grad[0].astype(F32)
    both = grad_f * gate_f
    out[0] = (normed * g * gate_f).astype(BF16)
    gate_grad[0] = (grad_f * normed * g).astype(BF16)
    ng = both * g
    mean = jnp.mean(normed * ng, axis=1, keepdims=True)
    attn_grad[:ROWS, :] = (inv * (ng - normed * mean)).astype(BF16)
    part = jnp.sum(both * normed, axis=0, keepdims=True)
    high = part.astype(BF16).astype(F32)
    line = lax.broadcasted_iota(jnp.int32, (EXTRA, HD), 0)
    extra = jnp.where(line == 0, high, jnp.where(line == 1, part - high, 0.0))
    attn_grad[ROWS:, :] = extra.astype(BF16)


def backward_kernel(place, ends, qseg, segs, q, da, *rest):
    kv, (keep, send, part, dkv, acc, dk, dv) = rest[: RING + 1], rest[RING + 1 :]
    acc[...] = jnp.zeros_like(acc)
    extra = [da[i, ROWS:, :].astype(F32) for i in range(QUAD)]
    terms = [rows[0:1] + rows[1:2] for rows in extra]
    part[...] = (terms[0] + terms[1]) + (terms[2] + terms[3])
    for pair in range(len(PAIRS)):
        blocks = key_blocks(place[0], pair)
        dk[...] = jnp.zeros_like(dk)
        dv[...] = jnp.zeros_like(dv)
        for c in range(TILE // CHUNK):

            @pl.when(meets(ends, place[0], c, blocks))
            def _(pair=pair, blocks=blocks, c=c):
                rows = slice(c * CHUNK, (c + 1) * CHUNK)
                same = same_history(qseg, segs, rows, blocks)
                for h in range(HEADS):
                    keys, values = pair_of(kv, pair, 0, h), pair_of(kv, pair, 1, h)
                    qb = queries_of(q, c, h)
                    db = da[2 * c : 2 * c + 2, :ROWS, head(h)].reshape(CHUNK, HSIZE)
                    half = dot(qb, keys, NT) * (0.5 * SCALE)
                    vd = dot(db, values, NT)
                    t = jnp.tanh(half)
                    w = jnp.where(same, half + half * t, 0.0).astype(BF16)
                    slope = (0.5 * SCALE) * vd * (1.0 + t) * (1.0 + half * (1.0 - t))
                    slope = jnp.where(same, slope, 0.0).astype(BF16)
                    acc[rows, head(h)] += dot(slope, keys, NN)
                    dk[:, head(h)] += dot(slope, qb, TN)
                    dv[:, head(h)] += dot(w, db, TN)

        for i, block in enumerate(blocks):
            rows = slice(i * ROWS, (i + 1) * ROWS)
            at = pl.multiple_of((block // QUAD) * (2 * ROWS), 2 * ROWS)
            dkv[pl.ds(at, ROWS), :] = dk[rows, :].astype(BF16)
            dkv[pl.ds(at + ROWS, ROWS), :] = dv[rows, :].astype(BF16)

    share_out(place[0], acc, keep, send)


def call(kernel, name, outs, operands, scalars=0, scratch=(), us=1):
    return pl.pallas_call(
        kernel,
        out_shape=tuple(jax.ShapeDtypeStruct(shape, dtype) for shape, dtype in outs),
        in_specs=[pl.BlockSpec(memory_space=pltpu.SMEM)] * scalars
        + [pl.BlockSpec(memory_space=pltpu.VMEM)] * (len(operands) - scalars),
        out_specs=(pl.BlockSpec(memory_space=pltpu.VMEM),) * len(outs),
        scratch_shapes=[pltpu.VMEM(shape, F32) for shape in scratch],
        compiler_params=pltpu.CompilerParams(vmem_limit_bytes=VMEM_LIMIT),
        cost_estimate=pl.CostEstimate(
            flops=us * 500_000_000, bytes_accessed=us * 1_000_000, transcendentals=0
        ),
        name=name,
    )(*operands)


def after(value, *others):
    return lax.optimization_barrier((value, *others))[0]


def sum_quad(keep, send):
    keep = keep + swap(send, CORE).astype(F32)
    return keep[:ROWS], lax.all_gather(keep[ROWS:].astype(BF16), "ctx", axis_index_groups=ZPAIRS)


def per_device(queries, key_states, value_states, gate_states, out_grad, segment_ids, norm_gain):
    place = lax.axis_index("ctx").astype(jnp.int32)
    rows, tile, half = (1, ROWS, HD), (TILE, HD), (HALF, HD)
    kv = jnp.concatenate([key_states, value_states], axis=0)
    first, kv = lax.optimization_barrier((queries, kv))
    gathered = lax.all_gather(
        jnp.pad(first, ((0, 1), (0, 0), (0, 0))), "ctx", axis_index_groups=QUADS
    )

    up = down = kv
    blocks = [kv]
    for _ in range(2):
        up, down = along(up, 1), along(down, -1)
        blocks += [up, down]
    blocks += [along(up, 1), along(down, -1), along(up[:, :CUT], 2), along(down[:, CUT:], -2)]

    segs = segment_ids.reshape(CTX, ROWS)
    ends = segs[:, :: ROWS - 1]
    (qseg,) = call(
        segment_kernel, "query_segments", [((TILE, ROWS), jnp.int32)], (place[None], segs), 1
    )
    shared = (place[None], ends, qseg, segs, gathered)

    keep, send = call(
        forward_kernel,
        "forward_tile",
        [(half, F32), (half, BF16)],
        (*shared, *blocks),
        2,
        [tile],
        us=3,
    )
    mine, came = sum_quad(keep, send)
    layer_out, gate_grad, attn_grad = call(
        norm_kernel,
        "norm_rows",
        [(rows, BF16), (rows, BF16), ((ROWS + EXTRA, HD), BF16)],
        (place[None], mine, came, gate_states, out_grad, norm_gain[None, :]),
        1,
    )
    grads = lax.all_gather(attn_grad, "ctx", axis_index_groups=QUADS)

    keep, send, part, dkv = call(
        backward_kernel,
        "backward_tile",
        [(half, F32), (half, BF16), ((1, HD), F32), ((RING * 2 * ROWS, HD), BF16)],
        (*shared, grads, *blocks),
        2,
        [tile, half, half],
        us=9,
    )
    dkv_sum = lax.psum_scatter(dkv, "ctx", tiled=True, axis_index_groups=RINGS)
    mine, came = sum_quad(keep, send)
    came = lax.dynamic_index_in_dim(came, 1 - lax.rem(place, QUAD) // ZHI, 0, keepdims=False)
    query_grad = (mine + came.astype(F32)).astype(BF16)

    dp = lax.axis_size("dp")
    part = after(part, query_grad)
    part = jnp.sum(everywhere(part, "dp", None, dp), axis=0, keepdims=True)
    part = jnp.sum(everywhere(part, "ctx", RINGS, RING), axis=0)
    gain_grad = part / math.sqrt(dp * CTX * ROWS)

    return (
        layer_out,
        query_grad[None],
        dkv_sum[None, :ROWS],
        dkv_sum[None, ROWS:],
        gate_grad,
        gain_grad,
    )


def solution(mesh):
    rows = P("dp", "ctx", None)
    return jax.shard_map(
        per_device,
        mesh=mesh,
        in_specs=(rows, rows, rows, rows, rows, P("dp", None), P()),
        out_specs=(rows, rows, rows, rows, rows, P()),
        check_vma=False,
    )
```

```python
import math

import jax
import jax.numpy as jnp
from jax import lax
from jax.experimental import pallas as pl
from jax.experimental.pallas import tpu as pltpu
from jax.sharding import PartitionSpec as P

HEADS = 4
HSIZE = 128
HD = 512
ROWS = 128
QUAD = 4
RING = 8
CTX = QUAD * RING
TILE = QUAD * ROWS
HALF = TILE // 2
CUT = ROWS // 2
SCALE = HSIZE ** (-0.5)
CHUNK = 256
CORE, ZHI = 1, 2
NT = (((1,), (1,)), ((), ()))
NN = (((1,), (0,)), ((), ()))
TN = (((0,), (0,)), ((), ()))
VMEM_LIMIT = 16 * 1024 * 1024
BF16, F32 = jnp.bfloat16, jnp.float32
EXTRA = 16
PAIRS = (((0, 0), (-1, 1)), ((1, 2), (2, 4)), ((-2, 3), (-3, 5)), ((3, 6), (4, 7)))
QUADS = [[y * QUAD + c for c in range(QUAD)] for y in range(RING)]
CORES = [[y * QUAD + z * ZHI + c for c in range(2)] for y in range(RING) for z in range(2)]
ZPAIRS = [[y * QUAD + z * ZHI + c for z in range(2)] for y in range(RING) for c in range(2)]
RINGS = [[y * QUAD + c for y in range(RING)] for c in range(QUAD)]


def dot(left, right, dims):
    return lax.dot_general(left, right, dims, preferred_element_type=F32)


def along(value, step):
    return lax.ppermute(value, "ctx", [(i, (i + step * QUAD) % CTX) for i in range(CTX)])


def swap(value, flip):
    return lax.ppermute(value, "ctx", [(i, i ^ flip) for i in range(CTX)])


def everywhere(value, axis, groups, size):
    value = jnp.broadcast_to(value, (size,) + value.shape[1:])
    return lax.all_to_all(value, axis, 0, 0, tiled=True, axis_index_groups=groups)


def head(h):
    return slice(h * HSIZE, (h + 1) * HSIZE)


def pair_of(kv, pair, which, h):
    return jnp.concatenate([kv[at][which, :, head(h)] for _, at in PAIRS[pair]], axis=0)


def key_blocks(place, pair):
    return [lax.rem(place + (offset + RING) * QUAD, CTX) for offset, _ in PAIRS[pair]]


def meets(ends, place, c, blocks):
    first = (place // QUAD) * QUAD + c * (CHUNK // ROWS)
    low, high = ends[first, 0], ends[first + CHUNK // ROWS - 1, 1]
    hits = [(ends[block, 0] <= high) & (ends[block, 1] >= low) for block in blocks]
    return hits[0] | hits[1]


def same_history(qseg, segs, rows, blocks):
    krow = jnp.concatenate([segs[pl.ds(block, 1), :] for block in blocks], axis=1)
    return jnp.concatenate([qseg[rows, :]] * 2, axis=1) == krow


def rows_of(place, flip):
    quad = lax.rem(place, QUAD) ^ flip
    return pl.ds(pl.multiple_of(quad * ROWS, ROWS), ROWS)


def share_out(place, acc, keep, send):
    for i, flip in enumerate((0, ZHI)):
        rows = slice(i * ROWS, (i + 1) * ROWS)
        keep[rows, :] = acc[rows_of(place, flip), :]
        send[rows, :] = acc[rows_of(place, flip ^ CORE), :].astype(BF16)


def segment_rows(place, segs, qseg):
    first = (place[0] // QUAD) * QUAD
    for i in range(QUAD):
        row = segs[pl.ds(first + i, 1), :]
        qseg[i * ROWS : (i + 1) * ROWS, :] = jnp.broadcast_to(row, (ROWS, ROWS)).T


def queries_of(q, c, h):
    return q[2 * c : 2 * c + 2, :, head(h)].reshape(CHUNK, HSIZE)


def forward_pairs(pairs, place, ends, segs, q, kv, acc, qseg):
    segment_rows(place, segs, qseg)
    for pair in pairs:
        blocks = key_blocks(place[0], pair)
        for c in range(TILE // CHUNK):

            @pl.when(meets(ends, place[0], c, blocks))
            def _(pair=pair, blocks=blocks, c=c):
                rows = slice(c * CHUNK, (c + 1) * CHUNK)
                same = same_history(qseg, segs, rows, blocks)
                for h in range(HEADS):
                    keys, values = pair_of(kv, pair, 0, h), pair_of(kv, pair, 1, h)
                    half = dot(queries_of(q, c, h), keys, NT) * (0.5 * SCALE)
                    silu = half + half * jnp.tanh(half)
                    w = jnp.where(same, silu, 0.0).astype(BF16)
                    acc[rows, head(h)] += dot(w, values, NN)


def near_kernel(place, ends, segs, q, own, prev, next_, next2, acc, qseg):
    acc[...] = jnp.zeros_like(acc)
    kv = {0: own, 1: prev, 2: next_, 4: next2}
    forward_pairs((0, 1), place, ends, segs, q, kv, acc, qseg)


def far_kernel(place, ends, segs, q, begun, prev2, prev3, next3, low, high, *rest):
    keep, send, far, acc, qseg = rest
    far[:, :CUT, :] = low[...]
    far[:, CUT:, :] = high[...]
    acc[...] = begun[...]
    kv = {3: prev2, 5: prev3, 6: next3, 7: far}
    forward_pairs((2, 3), place, ends, segs, q, kv, acc, qseg)
    share_out(place[0], acc, keep, send)


def terms_of(part):
    high = part.astype(BF16).astype(F32)
    line = lax.broadcasted_iota(jnp.int32, (EXTRA, HD), 0)
    return jnp.where(line == 0, high, jnp.where(line == 1, part - high, 0.0)).astype(BF16)


def z_of(place):
    return lax.rem(place, QUAD) // ZHI


def norm_kernel(place, kept, came, gate, grad, product, gain, out, gate_grad, attn_grad):
    g = gain[...]
    other = came.at[1 - z_of(place[0])]
    for i in range(2):
        rows, theirs = slice(i * ROWS, (i + 1) * ROWS), slice((1 - i) * ROWS, (2 - i) * ROWS)
        att = kept[rows, :] + other[theirs, :].astype(F32)
        inv = lax.rsqrt(jnp.mean(att * att, axis=1, keepdims=True) + 1e-06)
        normed = att * inv
        if i == 0:
            gate_f = gate[0].astype(F32)
            grad_f = grad[0].astype(F32)
            both = grad_f * gate_f
            out[0] = (normed * g * gate_f).astype(BF16)
            gate_grad[0] = (grad_f * normed * g).astype(BF16)
            attn_grad[2 * ROWS :, :] = terms_of(jnp.sum(both * normed, axis=0, keepdims=True))
        else:
            both = product[...].astype(F32)
        ng = both * g
        mean = jnp.mean(normed * ng, axis=1, keepdims=True)
        attn_grad[rows, :] = (inv * (ng - normed * mean)).astype(BF16)


def backward_kernel(place, ends, segs, q, da, *rest):
    kv, (keep, send, extra, dkv, acc, dk, dv, qseg) = rest[:RING], rest[RING:]
    segment_rows(place, segs, qseg)
    acc[...] = jnp.zeros_like(acc)
    terms = [da[i, 2 * ROWS :, :].astype(F32) for i in range(2)]
    sums = [rows[0:1] + rows[1:2] for rows in terms]
    extra[...] = terms_of(sums[0] + sums[1])
    for pair in range(len(PAIRS)):
        blocks = key_blocks(place[0], pair)
        dk[...] = jnp.zeros_like(dk)
        dv[...] = jnp.zeros_like(dv)
        for c in range(TILE // CHUNK):

            @pl.when(meets(ends, place[0], c, blocks))
            def _(pair=pair, blocks=blocks, c=c):
                rows = slice(c * CHUNK, (c + 1) * CHUNK)
                same = same_history(qseg, segs, rows, blocks)
                at = pl.multiple_of((z_of(place[0]) ^ c) * ROWS, ROWS)
                for h in range(HEADS):
                    keys, values = pair_of(kv, pair, 0, h), pair_of(kv, pair, 1, h)
                    qb = queries_of(q, c, h)
                    db = da[:, pl.ds(at, ROWS), head(h)].reshape(CHUNK, HSIZE)
                    half = dot(qb, keys, NT) * (0.5 * SCALE)
                    vd = dot(db, values, NT)
                    t = jnp.tanh(half)
                    w = jnp.where(same, half + half * t, 0.0).astype(BF16)
                    slope = (0.5 * SCALE) * vd * (1.0 + t) * (1.0 + half * (1.0 - t))
                    slope = jnp.where(same, slope, 0.0).astype(BF16)
                    acc[rows, head(h)] += dot(slope, keys, NN)
                    dk[:, head(h)] += dot(slope, qb, TN)
                    dv[:, head(h)] += dot(w, db, TN)

        for i, block in enumerate(blocks):
            rows = slice(i * ROWS, (i + 1) * ROWS)
            at = pl.multiple_of((block // QUAD) * (2 * ROWS), 2 * ROWS)
            dkv[pl.ds(at, ROWS), :] = dk[rows, :].astype(BF16)
            dkv[pl.ds(at + ROWS, ROWS), :] = dv[rows, :].astype(BF16)

    share_out(place[0], acc, keep, send)


def call(kernel, name, outs, operands, scalars=0, scratch=(), us=1):
    return pl.pallas_call(
        kernel,
        out_shape=tuple(jax.ShapeDtypeStruct(shape, dtype) for shape, dtype in outs),
        in_specs=[pl.BlockSpec(memory_space=pltpu.SMEM)] * scalars
        + [pl.BlockSpec(memory_space=pltpu.VMEM)] * (len(operands) - scalars),
        out_specs=(pl.BlockSpec(memory_space=pltpu.VMEM),) * len(outs),
        scratch_shapes=[
            pltpu.VMEM(shape, jnp.int32 if shape[1] == ROWS else F32) for shape in scratch
        ],
        compiler_params=pltpu.CompilerParams(vmem_limit_bytes=VMEM_LIMIT),
        cost_estimate=pl.CostEstimate(
            flops=us * 500_000_000, bytes_accessed=us * 1_000_000, transcendentals=0
        ),
        name=name,
    )(*operands)


def after(value, *others):
    return lax.optimization_barrier((value, *others))[0]


def per_device(queries, key_states, value_states, gate_states, out_grad, segment_ids, norm_gain):
    place = lax.axis_index("ctx").astype(jnp.int32)
    rows, tile, half = (1, ROWS, HD), (TILE, HD), (HALF, HD)
    kv = jnp.concatenate([key_states, value_states], axis=0)
    first, kv = lax.optimization_barrier((queries, kv))
    product = (out_grad.astype(F32) * gate_states.astype(F32)).astype(BF16)
    gathered = lax.all_gather(
        jnp.concatenate([first, product], axis=0), "ctx", axis_index_groups=QUADS
    )

    up = down = kv
    blocks = [kv]
    for _ in range(2):
        up, down = along(up, 1), along(down, -1)
        blocks += [up, down]
    blocks += [along(up, 1), along(down, -1), along(up[:, :CUT], 2), along(down[:, CUT:], -2)]

    segs = segment_ids.reshape(CTX, ROWS)
    ends = segs[:, :: ROWS - 1]
    product = lax.dynamic_index_in_dim(gathered, lax.rem(place, QUAD) ^ ZHI, 0, keepdims=False)[1]
    shared = (place[None], ends, segs, gathered[:, 0])

    (begun,) = call(
        near_kernel,
        "forward_near",
        [(tile, F32)],
        (*shared, *(blocks[at] for at in (0, 1, 2, 4))),
        2,
        [(TILE, ROWS)],
        us=2,
    )
    keep, send, far = call(
        far_kernel,
        "forward_far",
        [(half, F32), (half, BF16), ((2, ROWS, HD), BF16)],
        (*shared, begun, *(blocks[at] for at in (3, 5, 6, 7, 8))),
        2,
        [tile, (TILE, ROWS)],
        us=2,
    )
    keep = keep + swap(send, CORE).astype(F32)
    came = lax.all_gather(keep.astype(BF16), "ctx", axis_index_groups=ZPAIRS)
    layer_out, gate_grad, attn_grad = call(
        norm_kernel,
        "norm_rows",
        [(rows, BF16), (rows, BF16), ((2 * ROWS + EXTRA, HD), BF16)],
        (place[None], keep, came, gate_states, out_grad, product, norm_gain[None, :]),
        1,
    )
    grads = lax.all_gather(attn_grad, "ctx", axis_index_groups=CORES)

    keep, send, extra, dkv = call(
        backward_kernel,
        "backward_tile",
        [(half, F32), (half, BF16), ((EXTRA, HD), BF16), ((RING * 2 * ROWS, HD), BF16)],
        (*shared, grads, *blocks[: RING - 1], far),
        2,
        [tile, half, half, (TILE, ROWS)],
        us=9,
    )
    dkv_sum = lax.psum_scatter(dkv, "ctx", tiled=True, axis_index_groups=RINGS)
    keep = keep + swap(send, CORE).astype(F32)
    send = jnp.concatenate([keep[ROWS:].astype(BF16), extra], axis=0)
    came = lax.all_gather(send, "ctx", axis_index_groups=ZPAIRS)
    theirs = lax.dynamic_index_in_dim(came, 1 - z_of(place), 0, keepdims=False)[:ROWS]
    query_grad = (keep[:ROWS] + theirs.astype(F32)).astype(BF16)

    dp = lax.axis_size("dp")
    part = jnp.sum(came[:, ROWS : ROWS + 2].astype(F32), axis=(0, 1))[None]
    part = jnp.sum(everywhere(part, "dp", None, dp), axis=0, keepdims=True)
    part = jnp.sum(everywhere(part, "ctx", RINGS, RING), axis=0)
    gain_grad = part / math.sqrt(dp * CTX * ROWS)

    return (
        layer_out,
        query_grad[None],
        dkv_sum[None, :ROWS],
        dkv_sum[None, ROWS:],
        gate_grad,
        gain_grad,
    )


def solution(mesh):
    rows = P("dp", "ctx", None)
    return jax.shard_map(
        per_device,
        mesh=mesh,
        in_specs=(rows, rows, rows, rows, rows, P("dp", None), P()),
        out_specs=(rows, rows, rows, rows, rows, P()),
        check_vma=False,
    )
```

```python
import math

import jax
import jax.numpy as jnp
from jax import lax
from jax.experimental import pallas as pl
from jax.experimental.pallas import tpu as pltpu
from jax.sharding import PartitionSpec as P

HEADS = 4
HSIZE = 128
HD = 512
ROWS = 128
QUAD = 4
RING = 8
CTX = QUAD * RING
TILE = QUAD * ROWS
HALF = TILE // 2
CUT = ROWS // 2
SCALE = HSIZE ** (-0.5)
CHUNK = 256
CORE, ZHI = 1, 2
NT = (((1,), (1,)), ((), ()))
NN = (((1,), (0,)), ((), ()))
TN = (((0,), (0,)), ((), ()))
VMEM_LIMIT = 16 * 1024 * 1024
BF16, F32 = jnp.bfloat16, jnp.float32
EXTRA = 16
PAIRS = (((0, 0), (-1, 1)), ((1, 2), (2, 4)), ((-2, 3), (-3, 5)), ((3, 6), (4, 7)))
QUADS = [[y * QUAD + c for c in range(QUAD)] for y in range(RING)]
CORES = [[y * QUAD + z * ZHI + c for c in range(2)] for y in range(RING) for z in range(2)]
ZPAIRS = [[y * QUAD + z * ZHI + c for z in range(2)] for y in range(RING) for c in range(2)]
RINGS = [[y * QUAD + c for y in range(RING)] for c in range(QUAD)]


def dot(left, right, dims):
    return lax.dot_general(left, right, dims, preferred_element_type=F32)


def along(value, step):
    return lax.ppermute(value, "ctx", [(i, (i + step * QUAD) % CTX) for i in range(CTX)])


def swap(value, flip):
    return lax.ppermute(value, "ctx", [(i, i ^ flip) for i in range(CTX)])


def everywhere(value, axis, groups, size):
    value = jnp.broadcast_to(value, (size,) + value.shape[1:])
    return lax.all_to_all(value, axis, 0, 0, tiled=True, axis_index_groups=groups)


def head(h):
    return slice(h * HSIZE, (h + 1) * HSIZE)


def pair_of(kv, pair, which, h):
    return jnp.concatenate([kv[at][which, :, head(h)] for _, at in PAIRS[pair]], axis=0)


def key_blocks(place, pair):
    return [lax.rem(place + (offset + RING) * QUAD, CTX) for offset, _ in PAIRS[pair]]


def meets(ends, place, c, blocks):
    first = (place // QUAD) * QUAD + c * (CHUNK // ROWS)
    low, high = ends[first, 0], ends[first + CHUNK // ROWS - 1, 1]
    hits = [(ends[block, 0] <= high) & (ends[block, 1] >= low) for block in blocks]
    return hits[0] | hits[1]


def same_history(qseg, segs, rows, blocks):
    krow = jnp.concatenate([segs[pl.ds(block, 1), :] for block in blocks], axis=1)
    return jnp.concatenate([qseg[rows, :]] * 2, axis=1) == krow


def rows_of(place, flip):
    quad = lax.rem(place, QUAD) ^ flip
    return pl.ds(pl.multiple_of(quad * ROWS, ROWS), ROWS)


def share_out(place, acc, keep, send):
    for i, flip in enumerate((0, ZHI)):
        rows = slice(i * ROWS, (i + 1) * ROWS)
        keep[rows, :] = acc[rows_of(place, flip), :]
        send[rows, :] = acc[rows_of(place, flip ^ CORE), :].astype(BF16)


def segment_rows(place, segs, qseg):
    first = (place[0] // QUAD) * QUAD
    for i in range(QUAD):
        row = segs[pl.ds(first + i, 1), :]
        qseg[i * ROWS : (i + 1) * ROWS, :] = jnp.broadcast_to(row, (ROWS, ROWS)).T


def queries_of(q, c, h):
    return q[2 * c : 2 * c + 2, :, head(h)].reshape(CHUNK, HSIZE)


def forward_pairs(pairs, place, ends, segs, q, kv, acc, qseg):
    segment_rows(place, segs, qseg)
    for pair in pairs:
        blocks = key_blocks(place[0], pair)
        for c in range(TILE // CHUNK):

            @pl.when(meets(ends, place[0], c, blocks))
            def _(pair=pair, blocks=blocks, c=c):
                rows = slice(c * CHUNK, (c + 1) * CHUNK)
                same = same_history(qseg, segs, rows, blocks)
                for h in range(HEADS):
                    keys, values = pair_of(kv, pair, 0, h), pair_of(kv, pair, 1, h)
                    half = dot(queries_of(q, c, h), keys, NT) * (0.5 * SCALE)
                    silu = half + half * jnp.tanh(half)
                    w = jnp.where(same, silu, 0.0).astype(BF16)
                    acc[rows, head(h)] += dot(w, values, NN)


def near_kernel(place, ends, segs, q, own, prev, next_, next2, acc, qseg):
    acc[...] = jnp.zeros_like(acc)
    kv = {0: own, 1: prev, 2: next_, 4: next2}
    forward_pairs((0, 1), place, ends, segs, q, kv, acc, qseg)


def far_kernel(place, ends, segs, q, begun, prev2, prev3, next3, low, high, *rest):
    keep, send, far, acc, qseg = rest
    far[:, :CUT, :] = low[...]
    far[:, CUT:, :] = high[...]
    acc[...] = begun[...]
    kv = {3: prev2, 5: prev3, 6: next3, 7: far}
    forward_pairs((2, 3), place, ends, segs, q, kv, acc, qseg)
    share_out(place[0], acc, keep, send)


def terms_of(part):
    high = part.astype(BF16).astype(F32)
    line = lax.broadcasted_iota(jnp.int32, (EXTRA, HD), 0)
    return jnp.where(line == 0, high, jnp.where(line == 1, part - high, 0.0)).astype(BF16)


def z_of(place):
    return lax.rem(place, QUAD) // ZHI


def norm_kernel(
    place, kept, came, gate, grad, gain, gathered, out, gate_grad, attn_grad, product, sem
):
    copy = pltpu.make_async_copy(
        gathered.at[lax.rem(place[0], QUAD) ^ ZHI, 1], product, sem
    )
    copy.start()
    g = gain[...]
    other = came.at[1 - z_of(place[0])]
    for i in range(2):
        rows, theirs = slice(i * ROWS, (i + 1) * ROWS), slice((1 - i) * ROWS, (2 - i) * ROWS)
        att = kept[rows, :] + other[theirs, :].astype(F32)
        inv = lax.rsqrt(jnp.mean(att * att, axis=1, keepdims=True) + 1e-06)
        normed = att * inv
        if i == 0:
            gate_f = gate[0].astype(F32)
            grad_f = grad[0].astype(F32)
            both = grad_f * gate_f
            out[0] = (normed * g * gate_f).astype(BF16)
            gate_grad[0] = (grad_f * normed * g).astype(BF16)
            attn_grad[2 * ROWS :, :] = terms_of(jnp.sum(both * normed, axis=0, keepdims=True))
        else:
            copy.wait()
            both = product[...].astype(F32)
        ng = both * g
        mean = jnp.mean(normed * ng, axis=1, keepdims=True)
        attn_grad[rows, :] = (inv * (ng - normed * mean)).astype(BF16)


def backward_kernel(place, ends, segs, q, da, *rest):
    kv, (keep, send, extra, dkv, acc, dk, dv, qseg) = rest[:RING], rest[RING:]
    segment_rows(place, segs, qseg)
    acc[...] = jnp.zeros_like(acc)
    terms = [da[i, 2 * ROWS :, :].astype(F32) for i in range(2)]
    sums = [rows[0:1] + rows[1:2] for rows in terms]
    extra[...] = terms_of(sums[0] + sums[1])
    for pair in range(len(PAIRS)):
        blocks = key_blocks(place[0], pair)
        dk[...] = jnp.zeros_like(dk)
        dv[...] = jnp.zeros_like(dv)
        for c in range(TILE // CHUNK):

            @pl.when(meets(ends, place[0], c, blocks))
            def _(pair=pair, blocks=blocks, c=c):
                rows = slice(c * CHUNK, (c + 1) * CHUNK)
                same = same_history(qseg, segs, rows, blocks)
                at = pl.multiple_of((z_of(place[0]) ^ c) * ROWS, ROWS)
                for h in range(HEADS):
                    keys, values = pair_of(kv, pair, 0, h), pair_of(kv, pair, 1, h)
                    qb = queries_of(q, c, h)
                    db = da[:, pl.ds(at, ROWS), head(h)].reshape(CHUNK, HSIZE)
                    half = dot(qb, keys, NT) * (0.5 * SCALE)
                    vd = dot(db, values, NT)
                    t = jnp.tanh(half)
                    w = jnp.where(same, half + half * t, 0.0).astype(BF16)
                    slope = (0.5 * SCALE) * vd * (1.0 + t) * (1.0 + half * (1.0 - t))
                    slope = jnp.where(same, slope, 0.0).astype(BF16)
                    acc[rows, head(h)] += dot(slope, keys, NN)
                    dk[:, head(h)] += dot(slope, qb, TN)
                    dv[:, head(h)] += dot(w, db, TN)

        for i, block in enumerate(blocks):
            rows = slice(i * ROWS, (i + 1) * ROWS)
            at = pl.multiple_of((block // QUAD) * (2 * ROWS), 2 * ROWS)
            dkv[pl.ds(at, ROWS), :] = dk[rows, :].astype(BF16)
            dkv[pl.ds(at + ROWS, ROWS), :] = dv[rows, :].astype(BF16)

    share_out(place[0], acc, keep, send)


def call(kernel, name, outs, operands, scalars=0, scratch=(), us=1):
    return pl.pallas_call(
        kernel,
        out_shape=tuple(jax.ShapeDtypeStruct(shape, dtype) for shape, dtype in outs),
        in_specs=[pl.BlockSpec(memory_space=pltpu.SMEM)] * scalars
        + [pl.BlockSpec(memory_space=pltpu.VMEM)] * (len(operands) - scalars),
        out_specs=(pl.BlockSpec(memory_space=pltpu.VMEM),) * len(outs),
        scratch_shapes=[
            pltpu.VMEM(shape, jnp.int32 if shape[1] == ROWS else F32) for shape in scratch
        ],
        compiler_params=pltpu.CompilerParams(vmem_limit_bytes=VMEM_LIMIT),
        cost_estimate=pl.CostEstimate(
            flops=us * 500_000_000, bytes_accessed=us * 1_000_000, transcendentals=0
        ),
        name=name,
    )(*operands)


def after(value, *others):
    return lax.optimization_barrier((value, *others))[0]


def per_device(queries, key_states, value_states, gate_states, out_grad, segment_ids, norm_gain):
    place = lax.axis_index("ctx").astype(jnp.int32)
    rows, tile, half = (1, ROWS, HD), (TILE, HD), (HALF, HD)
    kv = jnp.concatenate([key_states, value_states], axis=0)
    first, kv = lax.optimization_barrier((queries, kv))
    product = (out_grad.astype(F32) * gate_states.astype(F32)).astype(BF16)
    gathered = lax.all_gather(
        jnp.concatenate([first, product], axis=0), "ctx", axis_index_groups=QUADS
    )

    up = down = kv
    blocks = [kv]
    for _ in range(2):
        up, down = along(up, 1), along(down, -1)
        blocks += [up, down]
    blocks += [along(up, 1), along(down, -1), along(up[:, :CUT], 2), along(down[:, CUT:], -2)]

    segs = segment_ids.reshape(CTX, ROWS)
    ends = segs[:, :: ROWS - 1]
    shared = (place[None], ends, segs, gathered[:, 0])

    (begun,) = call(
        near_kernel,
        "forward_near",
        [(tile, F32)],
        (*shared, *(blocks[at] for at in (0, 1, 2, 4))),
        2,
        [(TILE, ROWS)],
        us=2,
    )
    keep, send, far = call(
        far_kernel,
        "forward_far",
        [(half, F32), (half, BF16), ((2, ROWS, HD), BF16)],
        (*shared, begun, *(blocks[at] for at in (3, 5, 6, 7, 8))),
        2,
        [tile, (TILE, ROWS)],
        us=2,
    )
    came = lax.all_gather(send, "ctx", axis_index_groups=CORES)
    keep = keep + lax.dynamic_index_in_dim(came, 1 - place % 2, 0, keepdims=False).astype(F32)
    came = lax.all_gather(keep.astype(BF16), "ctx", axis_index_groups=ZPAIRS)
    layer_out, gate_grad, attn_grad = pl.pallas_call(
        norm_kernel,
        out_shape=(
            jax.ShapeDtypeStruct(rows, BF16),
            jax.ShapeDtypeStruct(rows, BF16),
            jax.ShapeDtypeStruct((2 * ROWS + EXTRA, HD), BF16),
        ),
        in_specs=[pl.BlockSpec(memory_space=pltpu.SMEM)]
        + [pl.BlockSpec(memory_space=pltpu.VMEM)] * 5
        + [pl.BlockSpec(memory_space=pl.ANY)],
        out_specs=(pl.BlockSpec(memory_space=pltpu.VMEM),) * 3,
        scratch_shapes=[pltpu.VMEM((ROWS, HD), BF16), pltpu.SemaphoreType.DMA],
        compiler_params=pltpu.CompilerParams(vmem_limit_bytes=VMEM_LIMIT),
        cost_estimate=pl.CostEstimate(
            flops=500_000_000, bytes_accessed=1_000_000, transcendentals=0
        ),
        name="norm_rows",
    )(place[None], keep, came, gate_states, out_grad, norm_gain[None, :], gathered)
    grads = lax.all_gather(attn_grad, "ctx", axis_index_groups=CORES)

    keep, send, extra, dkv = call(
        backward_kernel,
        "backward_tile",
        [(half, F32), (half, BF16), ((EXTRA, HD), BF16), ((RING * 2 * ROWS, HD), BF16)],
        (*shared, grads, *blocks[: RING - 1], far),
        2,
        [tile, half, half, (TILE, ROWS)],
        us=9,
    )
    dkv_sum = lax.psum_scatter(dkv, "ctx", tiled=True, axis_index_groups=RINGS)
    keep = keep + swap(send, CORE).astype(F32)
    send = jnp.concatenate([keep[ROWS:].astype(BF16), extra], axis=0)
    came = lax.all_gather(send, "ctx", axis_index_groups=ZPAIRS)
    theirs = lax.dynamic_index_in_dim(came, 1 - z_of(place), 0, keepdims=False)[:ROWS]
    query_grad = (keep[:ROWS] + theirs.astype(F32)).astype(BF16)

    dp = lax.axis_size("dp")
    part = jnp.sum(came[:, ROWS : ROWS + 2].astype(F32), axis=(0, 1))[None]
    part = jnp.sum(everywhere(part, "dp", None, dp), axis=0, keepdims=True)
    part = jnp.sum(everywhere(part, "ctx", RINGS, RING), axis=0)
    gain_grad = part / math.sqrt(dp * CTX * ROWS)

    return (
        layer_out,
        query_grad[None],
        dkv_sum[None, :ROWS],
        dkv_sum[None, ROWS:],
        gate_grad,
        gain_grad,
    )


def solution(mesh):
    rows = P("dp", "ctx", None)
    return jax.shard_map(
        per_device,
        mesh=mesh,
        in_specs=(rows, rows, rows, rows, rows, P("dp", None), P()),
        out_specs=(rows, rows, rows, rows, rows, P()),
        check_vma=False,
    )
```

```python
import math

import jax
import jax.numpy as jnp
from jax import lax
from jax.experimental import pallas as pl
from jax.experimental.pallas import tpu as pltpu
from jax.sharding import PartitionSpec as P

HEADS = 4
HSIZE = 128
HD = 512
ROWS = 128
QUAD = 4
RING = 8
CTX = QUAD * RING
TILE = QUAD * ROWS
HALF = TILE // 2
CUT = ROWS // 2
SCALE = HSIZE ** (-0.5)
CHUNK = 256
CORE, ZHI = 1, 2
NT = (((1,), (1,)), ((), ()))
NN = (((1,), (0,)), ((), ()))
TN = (((0,), (0,)), ((), ()))
VMEM_LIMIT = 16 * 1024 * 1024
BF16, F32 = jnp.bfloat16, jnp.float32
EXTRA = 16
PAIRS = (((0, 0), (-1, 1)), ((1, 2), (2, 4)), ((-2, 3), (-3, 5)), ((3, 6), (4, 7)))
QUADS = [[y * QUAD + c for c in range(QUAD)] for y in range(RING)]
CORES = [[y * QUAD + z * ZHI + c for c in range(2)] for y in range(RING) for z in range(2)]
ZPAIRS = [[y * QUAD + z * ZHI + c for z in range(2)] for y in range(RING) for c in range(2)]
RINGS = [[y * QUAD + c for y in range(RING)] for c in range(QUAD)]


def dot(left, right, dims):
    return lax.dot_general(left, right, dims, preferred_element_type=F32)


def along(value, step):
    return lax.ppermute(value, "ctx", [(i, (i + step * QUAD) % CTX) for i in range(CTX)])


def swap(value, flip):
    return lax.ppermute(value, "ctx", [(i, i ^ flip) for i in range(CTX)])


def everywhere(value, axis, groups, size):
    value = jnp.broadcast_to(value, (size,) + value.shape[1:])
    return lax.all_to_all(value, axis, 0, 0, tiled=True, axis_index_groups=groups)


def head(h):
    return slice(h * HSIZE, (h + 1) * HSIZE)


def pair_of(kv, pair, which, h):
    return jnp.concatenate([kv[at][which, :, head(h)] for _, at in PAIRS[pair]], axis=0)


def key_blocks(place, pair):
    return [lax.rem(place + (offset + RING) * QUAD, CTX) for offset, _ in PAIRS[pair]]


def meets(ends, place, c, blocks):
    first = (place // QUAD) * QUAD + c * (CHUNK // ROWS)
    low, high = ends[first, 0], ends[first + CHUNK // ROWS - 1, 1]
    hits = [(ends[block, 0] <= high) & (ends[block, 1] >= low) for block in blocks]
    return hits[0] | hits[1]


def same_history(qseg, segs, rows, blocks):
    krow = jnp.concatenate([segs[pl.ds(block, 1), :] for block in blocks], axis=1)
    return jnp.concatenate([qseg[rows, :]] * 2, axis=1) == krow


def rows_of(place, flip):
    quad = lax.rem(place, QUAD) ^ flip
    return pl.ds(pl.multiple_of(quad * ROWS, ROWS), ROWS)


def share_out(place, acc, keep, send):
    for i, flip in enumerate((0, ZHI)):
        rows = slice(i * ROWS, (i + 1) * ROWS)
        keep[rows, :] = acc[rows_of(place, flip), :]
        send[rows, :] = acc[rows_of(place, flip ^ CORE), :].astype(BF16)


def segment_rows(place, segs, qseg):
    first = (place[0] // QUAD) * QUAD
    for i in range(QUAD):
        row = segs[pl.ds(first + i, 1), :]
        qseg[i * ROWS : (i + 1) * ROWS, :] = jnp.broadcast_to(row, (ROWS, ROWS)).T


def queries_of(q, c, h):
    return q[2 * c : 2 * c + 2, :, head(h)].reshape(CHUNK, HSIZE)


def forward_pairs(pairs, place, ends, segs, q, kv, acc, qseg):
    segment_rows(place, segs, qseg)
    for pair in pairs:
        blocks = key_blocks(place[0], pair)
        for c in range(TILE // CHUNK):

            @pl.when(meets(ends, place[0], c, blocks))
            def _(pair=pair, blocks=blocks, c=c):
                rows = slice(c * CHUNK, (c + 1) * CHUNK)
                same = same_history(qseg, segs, rows, blocks)
                for h in range(HEADS):
                    keys, values = pair_of(kv, pair, 0, h), pair_of(kv, pair, 1, h)
                    half = dot(queries_of(q, c, h), keys, NT) * (0.5 * SCALE)
                    silu = half + half * jnp.tanh(half)
                    w = jnp.where(same, silu, 0.0).astype(BF16)
                    acc[rows, head(h)] += dot(w, values, NN)


def near_kernel(place, ends, segs, q, own, prev, next_, next2, acc, qseg):
    acc[...] = jnp.zeros_like(acc)
    kv = {0: own, 1: prev, 2: next_, 4: next2}
    forward_pairs((0, 1), place, ends, segs, q, kv, acc, qseg)


def far_kernel(place, ends, segs, q, begun, prev2, prev3, next3, low, high, *rest):
    keep, send, far, acc, qseg = rest
    far[:, :CUT, :] = low[...]
    far[:, CUT:, :] = high[...]
    acc[...] = begun[...]
    kv = {3: prev2, 5: prev3, 6: next3, 7: far}
    forward_pairs((2, 3), place, ends, segs, q, kv, acc, qseg)
    share_out(place[0], acc, keep, send)


def terms_of(part):
    high = part.astype(BF16).astype(F32)
    line = lax.broadcasted_iota(jnp.int32, (EXTRA, HD), 0)
    return jnp.where(line == 0, high, jnp.where(line == 1, part - high, 0.0)).astype(BF16)


def z_of(place):
    return lax.rem(place, QUAD) // ZHI


def norm_kernel(
    place, kept, came, gate, grad, gain, gathered, out, gate_grad, attn_grad, product, sem
):
    copy = pltpu.make_async_copy(
        gathered.at[lax.rem(place[0], QUAD) ^ ZHI, 1], product, sem
    )
    copy.start()
    g = gain[...]
    other = came.at[1 - z_of(place[0])]
    for i in range(2):
        rows, theirs = slice(i * ROWS, (i + 1) * ROWS), slice((1 - i) * ROWS, (2 - i) * ROWS)
        att = kept[rows, :] + other[theirs, :].astype(F32)
        inv = lax.rsqrt(jnp.mean(att * att, axis=1, keepdims=True) + 1e-06)
        normed = att * inv
        if i == 0:
            gate_f = gate[0].astype(F32)
            grad_f = grad[0].astype(F32)
            both = grad_f * gate_f
            out[0] = (normed * g * gate_f).astype(BF16)
            gate_grad[0] = (grad_f * normed * g).astype(BF16)
            attn_grad[2 * ROWS :, :] = terms_of(jnp.sum(both * normed, axis=0, keepdims=True))
        else:
            copy.wait()
            both = product[...].astype(F32)
        ng = both * g
        mean = jnp.mean(normed * ng, axis=1, keepdims=True)
        attn_grad[rows, :] = (inv * (ng - normed * mean)).astype(BF16)


def backward_kernel(place, ends, segs, q, da, *rest):
    kv, (keep, send, extra, dkv, acc, dk, dv, qseg, out, sems) = rest[:RING], rest[RING:]
    copies = []
    segment_rows(place, segs, qseg)
    acc[...] = jnp.zeros_like(acc)
    terms = [da[i, 2 * ROWS :, :].astype(F32) for i in range(2)]
    sums = [rows[0:1] + rows[1:2] for rows in terms]
    extra[...] = terms_of(sums[0] + sums[1])
    for pair in range(len(PAIRS)):
        blocks = key_blocks(place[0], pair)
        dk[...] = jnp.zeros_like(dk)
        dv[...] = jnp.zeros_like(dv)
        for c in range(TILE // CHUNK):

            @pl.when(meets(ends, place[0], c, blocks))
            def _(pair=pair, blocks=blocks, c=c):
                rows = slice(c * CHUNK, (c + 1) * CHUNK)
                same = same_history(qseg, segs, rows, blocks)
                at = pl.multiple_of((z_of(place[0]) ^ c) * ROWS, ROWS)
                for h in range(HEADS):
                    keys, values = pair_of(kv, pair, 0, h), pair_of(kv, pair, 1, h)
                    qb = queries_of(q, c, h)
                    db = da[:, pl.ds(at, ROWS), head(h)].reshape(CHUNK, HSIZE)
                    half = dot(qb, keys, NT) * (0.5 * SCALE)
                    vd = dot(db, values, NT)
                    t = jnp.tanh(half)
                    w = jnp.where(same, half + half * t, 0.0).astype(BF16)
                    slope = (0.5 * SCALE) * vd * (1.0 + t) * (1.0 + half * (1.0 - t))
                    slope = jnp.where(same, slope, 0.0).astype(BF16)
                    acc[rows, head(h)] += dot(slope, keys, NN)
                    dk[:, head(h)] += dot(slope, qb, TN)
                    dv[:, head(h)] += dot(w, db, TN)

        for i, block in enumerate(blocks):
            rows = slice(i * ROWS, (i + 1) * ROWS)
            at = pl.multiple_of((block // QUAD) * (2 * ROWS), 2 * ROWS)
            slot = 2 * pair + i
            out[slot, :ROWS, :] = dk[rows, :].astype(BF16)
            out[slot, ROWS:, :] = dv[rows, :].astype(BF16)
            copies.append(
                pltpu.make_async_copy(out.at[slot], dkv.at[pl.ds(at, 2 * ROWS)], sems.at[slot])
            )
            copies[-1].start()

    share_out(place[0], acc, keep, send)
    for copy in copies:
        copy.wait()


def call(kernel, name, outs, operands, scalars=0, scratch=(), us=1):
    return pl.pallas_call(
        kernel,
        out_shape=tuple(jax.ShapeDtypeStruct(shape, dtype) for shape, dtype in outs),
        in_specs=[pl.BlockSpec(memory_space=pltpu.SMEM)] * scalars
        + [pl.BlockSpec(memory_space=pltpu.VMEM)] * (len(operands) - scalars),
        out_specs=(pl.BlockSpec(memory_space=pltpu.VMEM),) * len(outs),
        scratch_shapes=[
            pltpu.VMEM(shape, jnp.int32 if shape[1] == ROWS else F32) for shape in scratch
        ],
        compiler_params=pltpu.CompilerParams(vmem_limit_bytes=VMEM_LIMIT),
        cost_estimate=pl.CostEstimate(
            flops=us * 500_000_000, bytes_accessed=us * 1_000_000, transcendentals=0
        ),
        name=name,
    )(*operands)


def after(value, *others):
    return lax.optimization_barrier((value, *others))[0]


def per_device(queries, key_states, value_states, gate_states, out_grad, segment_ids, norm_gain):
    place = lax.axis_index("ctx").astype(jnp.int32)
    rows, tile, half = (1, ROWS, HD), (TILE, HD), (HALF, HD)
    kv = jnp.concatenate([key_states, value_states], axis=0)
    first, kv = lax.optimization_barrier((queries, kv))
    product = (out_grad.astype(F32) * gate_states.astype(F32)).astype(BF16)
    gathered = lax.all_gather(
        jnp.concatenate([first, product], axis=0), "ctx", axis_index_groups=QUADS
    )

    up = down = kv
    blocks = [kv]
    for _ in range(2):
        up, down = along(up, 1), along(down, -1)
        blocks += [up, down]
    blocks += [along(up, 1), along(down, -1), along(up[:, :CUT], 2), along(down[:, CUT:], -2)]

    segs = segment_ids.reshape(CTX, ROWS)
    ends = segs[:, :: ROWS - 1]
    shared = (place[None], ends, segs, gathered[:, 0])

    (begun,) = call(
        near_kernel,
        "forward_near",
        [(tile, F32)],
        (*shared, *(blocks[at] for at in (0, 1, 2, 4))),
        2,
        [(TILE, ROWS)],
        us=2,
    )
    keep, send, far = call(
        far_kernel,
        "forward_far",
        [(half, F32), (half, BF16), ((2, ROWS, HD), BF16)],
        (*shared, begun, *(blocks[at] for at in (3, 5, 6, 7, 8))),
        2,
        [tile, (TILE, ROWS)],
        us=2,
    )
    came = lax.all_gather(send, "ctx", axis_index_groups=CORES)
    keep = keep + lax.dynamic_index_in_dim(came, 1 - place % 2, 0, keepdims=False).astype(F32)
    came = lax.all_gather(keep.astype(BF16), "ctx", axis_index_groups=ZPAIRS)
    layer_out, gate_grad, attn_grad = pl.pallas_call(
        norm_kernel,
        out_shape=(
            jax.ShapeDtypeStruct(rows, BF16),
            jax.ShapeDtypeStruct(rows, BF16),
            jax.ShapeDtypeStruct((2 * ROWS + EXTRA, HD), BF16),
        ),
        in_specs=[pl.BlockSpec(memory_space=pltpu.SMEM)]
        + [pl.BlockSpec(memory_space=pltpu.VMEM)] * 5
        + [pl.BlockSpec(memory_space=pl.ANY)],
        out_specs=(pl.BlockSpec(memory_space=pltpu.VMEM),) * 3,
        scratch_shapes=[pltpu.VMEM((ROWS, HD), BF16), pltpu.SemaphoreType.DMA],
        compiler_params=pltpu.CompilerParams(vmem_limit_bytes=VMEM_LIMIT),
        cost_estimate=pl.CostEstimate(
            flops=500_000_000, bytes_accessed=1_000_000, transcendentals=0
        ),
        name="norm_rows",
    )(place[None], keep, came, gate_states, out_grad, norm_gain[None, :], gathered)
    grads = lax.all_gather(attn_grad, "ctx", axis_index_groups=CORES)

    outs = [(half, F32), (half, BF16), ((EXTRA, HD), BF16), ((RING * 2 * ROWS, HD), BF16)]
    keep, send, extra, dkv = pl.pallas_call(
        backward_kernel,
        out_shape=tuple(jax.ShapeDtypeStruct(shape, dtype) for shape, dtype in outs),
        in_specs=[pl.BlockSpec(memory_space=pltpu.SMEM)] * 2
        + [pl.BlockSpec(memory_space=pltpu.VMEM)] * (3 + RING),
        out_specs=(pl.BlockSpec(memory_space=pltpu.VMEM),) * 3
        + (pl.BlockSpec(memory_space=pl.ANY),),
        scratch_shapes=[
            pltpu.VMEM(tile, F32),
            pltpu.VMEM(half, F32),
            pltpu.VMEM(half, F32),
            pltpu.VMEM((TILE, ROWS), jnp.int32),
            pltpu.VMEM((RING, 2 * ROWS, HD), BF16),
            pltpu.SemaphoreType.DMA((RING,)),
        ],
        compiler_params=pltpu.CompilerParams(vmem_limit_bytes=VMEM_LIMIT),
        cost_estimate=pl.CostEstimate(
            flops=4_500_000_000, bytes_accessed=9_000_000, transcendentals=0
        ),
        name="backward_tile",
    )(*shared, grads, *blocks[: RING - 1], far)
    dkv_sum = lax.psum_scatter(dkv, "ctx", tiled=True, axis_index_groups=RINGS)
    keep = keep + swap(send, CORE).astype(F32)
    send = jnp.concatenate([keep[ROWS:].astype(BF16), extra], axis=0)
    came = lax.all_gather(send, "ctx", axis_index_groups=ZPAIRS)
    theirs = lax.dynamic_index_in_dim(came, 1 - z_of(place), 0, keepdims=False)[:ROWS]
    query_grad = (keep[:ROWS] + theirs.astype(F32)).astype(BF16)

    dp = lax.axis_size("dp")
    part = jnp.sum(came[:, ROWS : ROWS + 2].astype(F32), axis=(0, 1))[None]
    part = jnp.sum(everywhere(part, "dp", None, dp), axis=0, keepdims=True)
    part = jnp.sum(everywhere(part, "ctx", RINGS, RING), axis=0)
    gain_grad = part / math.sqrt(dp * CTX * ROWS)

    return (
        layer_out,
        query_grad[None],
        dkv_sum[None, :ROWS],
        dkv_sum[None, ROWS:],
        gate_grad,
        gain_grad,
    )


def solution(mesh):
    rows = P("dp", "ctx", None)
    return jax.shard_map(
        per_device,
        mesh=mesh,
        in_specs=(rows, rows, rows, rows, rows, P("dp", None), P()),
        out_specs=(rows, rows, rows, rows, rows, P()),
        check_vma=False,
    )
```
